32 devices in a mesh: row: 4 (over y, x), col: 8 (over z, core).
Axes of the slice: x: 2, y: 2, z: 4, core: 2. Of those that a mesh axis runs over, the one named last changes fastest.
Arguments:
- matrix: float32 [16384, 16384], P('row', 'col'), may hold values from -6 to 6
- factor_inverse: float32 [512, 512], replicated, may hold values from -0.25 to 0.25
- panel: int32 [1], replicated, may hold values from 0 to 31
- split_index: int32 [1], replicated, may hold values from 4096 to 12288
Outputs:
- halves: float32 [16384, 512], P('col')
The draws below stay inside these ranges and needn't reach their ends.
All inputs are finite; a program needn't handle non-finite values.
Results may differ from the reference program's by a relative error of at most 0.000071.
Values sent between devices are 32-bit elements; how exact they have to be, the bound alone decides.
A program may use at most 128 MiB of HBM per device.

```python
import jax
import jax.numpy as jnp
from jax import lax

N = 16384
B = 512


def levels(key, extent, cuts, low, high):
    factor_of = 1.0
    for dim, parts in cuts:
        draws = jax.random.uniform(jax.random.fold_in(jax.random.fold_in(key, 6), dim), (parts,), jnp.float32, low / len(cuts), high / len(cuts))
        factor_of = factor_of * jnp.repeat(jnp.exp(draws), extent[dim] // parts).reshape((-1,) + (1,) * (len(extent) - 1 - dim))
    return factor_of


def gaussian(own_key, shape, width, limit, split=(), kind=jnp.bfloat16):
    gain = levels(own_key, shape, split, -0.22, 0.18) if split else 1.0
    drawn = jax.random.normal(own_key, shape, jnp.float32) * width * gain
    return jnp.minimum(jnp.maximum(drawn, -limit), limit).astype(kind)


def setup_inputs(seed: int = 0) -> dict:
    key_of = jax.random.split(jax.random.key(seed), 5)
    matrix = gaussian(key_of[0], (N, N), 1.0, 6.0, ((0, 4), (1, 8)), jnp.float32)
    factor_inverse = gaussian(key_of[1], (B, B), B ** -0.5, 0.25, (), jnp.float32)
    panel = jax.random.randint(key_of[2], (1,), 0, N // B).astype(jnp.int32)
    split_index = jax.random.randint(key_of[3], (1,), N // 4, 3 * N // 4 + 1).astype(jnp.int32)
    return dict(matrix=matrix, factor_inverse=factor_inverse, panel=panel, split_index=split_index)


def reference(matrix, factor_inverse, panel, split_index):
    start = panel[0] * B
    ident = (jnp.arange(N, dtype=jnp.int32)[:, None] == start + jnp.arange(B, dtype=jnp.int32)[None, :]).astype(jnp.float32)
    columns = lax.dynamic_slice_in_dim(matrix, start.astype(jnp.int32), B, 1)
    gram = lax.dot_general(matrix, columns, (((0,), (0,)), ((), ())), precision=lax.Precision.HIGHEST, preferred_element_type=jnp.float32) / N + ident
    factor = lax.dot_general(gram, factor_inverse, (((1,), (1,)), ((), ())), precision=lax.Precision.HIGHEST, preferred_element_type=jnp.float32)
    projector = 0.5 * (ident + jnp.dot(matrix, factor, precision=lax.Precision.HIGHEST, preferred_element_type=jnp.float32))
    index = jnp.arange(N, dtype=jnp.int32)
    keep = (index < N // 2) == (index < split_index[0])
    return jnp.where(keep[:, None], projector, jnp.float32(0.0))
```

```python
import functools

import jax
import jax.numpy as jnp
from jax import lax
from jax.experimental import pallas as pl
from jax.experimental.pallas import tpu as pltpu
from jax.sharding import PartitionSpec as P

GROUPS = 2
CHUNKS = 16
VMEM_LIMIT = 40 * 1024 * 1024


def remote(src, dst, send, recv, target):
    return pltpu.make_async_remote_copy(
        src_ref=src,
        dst_ref=dst,
        send_sem=send,
        recv_sem=recv,
        device_id=target,
        device_id_type=pl.DeviceIdType.MESH,
    )


def signal(barrier, target):
    pl.semaphore_signal(barrier, inc=1, device_id=target, device_id_type=pl.DeviceIdType.MESH)


def spread_kernel(
    line, chunk, x_ref, o_ref, ex, rin, lin,
    ex_send, ex_recv, r_send, r_recv, l_send, l_recv, s_send, s_recv,
):
    c = lax.axis_index("col")
    z = c // 2
    k = c % 2
    half = CHUNKS * chunk
    base = pl.multiple_of(k * half, half)
    other = pl.multiple_of((1 - k) * half, half)
    sibling, up, down = {"col": c + 1 - 2 * k}, {"col": c + 2}, {"col": c - 2}
    has_down, has_up = z > 0, z < line - 1

    barrier = pltpu.get_barrier_semaphore()
    signal(barrier, sibling)

    @pl.when(has_down)
    def _():
        signal(barrier, down)

    @pl.when(has_up)
    def _():
        signal(barrier, up)

    pl.semaphore_wait(barrier, 1 + has_down.astype(jnp.int32) + has_up.astype(jnp.int32))

    swap = remote(x_ref.at[pl.ds(other, half)], ex, ex_send, ex_recv, sibling)
    swap.start()
    swap.wait()

    def rows_of(i):
        return pl.ds(pl.multiple_of(i * chunk, chunk), chunk)

    def whole_rows(i):
        return pl.ds(pl.multiple_of(base + i * chunk, chunk), chunk)

    def up_copy(i):
        return remote(rin.at[rows_of(i)], rin.at[rows_of(i)], r_send.at[i], r_recv.at[i], up)

    def down_copy(i):
        return remote(lin.at[rows_of(i)], lin.at[rows_of(i)], l_send.at[i], l_recv.at[i], down)

    def side_copy(i):
        return remote(
            o_ref.at[whole_rows(i)], o_ref.at[whole_rows(i)], s_send.at[i], s_recv.at[i], sibling
        )

    def own(i):
        return x_ref[whole_rows(i), :] + ex[rows_of(i), :]

    last = jnp.maximum(z, line - 1 - z)

    def step(t, carry):
        i = t - z

        @pl.when((i >= 0) & (i < CHUNKS))
        def _():
            @pl.when(z == 0)
            def _():
                rin[rows_of(i), :] = own(i)

            @pl.when(has_down)
            def _():
                up_copy(i).wait_recv()
                rin[rows_of(i), :] = rin[rows_of(i), :] + own(i)

            @pl.when(has_up)
            def _():
                up_copy(i).start()

        j = t - (line - 1 - z)

        @pl.when((j >= 0) & (j < CHUNKS))
        def _():
            @pl.when(z == line - 1)
            def _():
                lin[rows_of(j), :] = own(j)

            @pl.when(has_up)
            def _():
                down_copy(j).wait_recv()
                lin[rows_of(j), :] = lin[rows_of(j), :] + own(j)

            @pl.when(has_down)
            def _():
                down_copy(j).start()

        m = t - last

        @pl.when((m >= 0) & (m < CHUNKS))
        def _():
            o_ref[whole_rows(m), :] = (rin[rows_of(m), :] + lin[rows_of(m), :]) - own(m)
            side_copy(m).start()

        return carry

    lax.fori_loop(0, CHUNKS + line - 1, step, 0)

    def finish(i, carry):
        @pl.when(has_up)
        def _():
            up_copy(i).wait_send()

        @pl.when(has_down)
        def _():
            down_copy(i).wait_send()

        side_copy(i).wait_send()
        remote(
            o_ref.at[pl.ds(pl.multiple_of(other + i * chunk, chunk), chunk)],
            o_ref.at[pl.ds(pl.multiple_of(other + i * chunk, chunk), chunk)],
            s_send.at[i], s_recv.at[i], sibling,
        ).wait_recv()
        return carry

    lax.fori_loop(0, CHUNKS, finish, 0)


def spread(x, line):
    rows, cols = x.shape
    half = rows // 2
    chunk = half // CHUNKS
    buffer = pltpu.VMEM((half, cols), jnp.float32)
    return pl.pallas_call(
        functools.partial(spread_kernel, line, chunk),
        out_shape=jax.ShapeDtypeStruct((rows, cols), jnp.float32),
        in_specs=[pl.BlockSpec(memory_space=pltpu.VMEM)],
        out_specs=pl.BlockSpec(memory_space=pltpu.VMEM),
        scratch_shapes=[buffer] * 3
        + [pltpu.SemaphoreType.DMA] * 2
        + [pltpu.SemaphoreType.DMA((CHUNKS,))] * 6,
        compiler_params=pltpu.CompilerParams(
            collective_id=1, has_side_effects=True, vmem_limit_bytes=VMEM_LIMIT
        ),
        cost_estimate=pl.CostEstimate(flops=0, bytes_accessed=160 * 1000000, transcendentals=0),
        name="spread_panel",
    )(x)


def collect_kernel(
    line, chunk, p_ref, o_ref, ex, rin, lin,
    ex_send, ex_recv, z_send, r_recv, l_recv, a_send, b_send, o_recv, *more_send,
):
    r = lax.axis_index("row")
    c = lax.axis_index("col")
    z = c // 2
    k = c % 2
    half = CHUNKS * chunk
    base = pl.multiple_of(k * half, half)
    other = pl.multiple_of((1 - k) * half, half)
    sibling, up, down = {"col": c + 1 - 2 * k}, {"col": c + 2}, {"col": c - 2}
    square = line == 4
    is_root = r == z
    if square:
        across_x, across_y = {"row": r + 1 - 2 * (r % 2)}, {"row": r + 2 - 4 * (r // 2)}
        same_x, same_y = (r % 2) == (z % 2), (r // 2) == (z // 2)
        is_x = jnp.logical_not(same_x) & same_y
        is_y = same_x & jnp.logical_not(same_y)
        is_far = jnp.logical_not(same_x) & jnp.logical_not(same_y)

    barrier = pltpu.get_barrier_semaphore()
    signal(barrier, sibling)

    @pl.when((z > 0) & (z <= r))
    def _():
        signal(barrier, down)

    @pl.when((z < line - 1) & (z >= r))
    def _():
        signal(barrier, up)

    if square:
        @pl.when(is_x | is_far)
        def _():
            signal(barrier, across_x)

        @pl.when(is_y | is_far)
        def _():
            signal(barrier, across_y)
    else:
        @pl.when(jnp.logical_not(is_root))
        def _():
            signal(barrier, {"row": z})

    if square:
        pl.semaphore_wait(barrier, jnp.where(is_far, 2, 3))
    else:
        pl.semaphore_wait(barrier, jnp.where(is_root, line, 2))

    swap = remote(p_ref.at[pl.ds(other, half)], ex, ex_send, ex_recv, sibling)
    swap.start()
    swap.wait()

    def rows_of(i):
        return pl.ds(pl.multiple_of(i * chunk, chunk), chunk)

    def own(i):
        return p_ref[pl.ds(pl.multiple_of(base + i * chunk, chunk), chunk), :] + ex[rows_of(i), :]

    def up_copy(i):
        return remote(rin.at[rows_of(i)], rin.at[rows_of(i)], z_send.at[i], r_recv.at[i], up)

    def down_copy(i):
        return remote(lin.at[rows_of(i)], lin.at[rows_of(i)], z_send.at[i], l_recv.at[i], down)

    def out_copy(i, sems, target):
        return remote(o_ref.at[rows_of(i)], o_ref.at[rows_of(i)], sems.at[i], o_recv.at[i], target)

    last = jnp.maximum(z, line - 1 - z)

    def within(i):
        return (i >= 0) & (i < CHUNKS)

    def step(t, carry):
        i = t - z

        @pl.when(within(i) & (z < r))
        def _():
            @pl.when(z == 0)
            def _():
                rin[rows_of(i), :] = own(i)

            @pl.when(z > 0)
            def _():
                up_copy(i).wait_recv()
                rin[rows_of(i), :] = rin[rows_of(i), :] + own(i)

            up_copy(i).start()

        j = t - (line - 1 - z)

        @pl.when(within(j) & (z > r))
        def _():
            @pl.when(z == line - 1)
            def _():
                lin[rows_of(j), :] = own(j)

            @pl.when(z < line - 1)
            def _():
                down_copy(j).wait_recv()
                lin[rows_of(j), :] = lin[rows_of(j), :] + own(j)

            down_copy(j).start()

        m = t - last

        @pl.when(within(m) & is_root)
        def _():
            o_ref[rows_of(m), :] = own(m)

            @pl.when(z > 0)
            def _():
                up_copy(m).wait_recv()
                o_ref[rows_of(m), :] = o_ref[rows_of(m), :] + rin[rows_of(m), :]

            @pl.when(z < line - 1)
            def _():
                down_copy(m).wait_recv()
                o_ref[rows_of(m), :] = o_ref[rows_of(m), :] + lin[rows_of(m), :]

            if square:
                out_copy(m, a_send, across_x).start()
                out_copy(m, b_send, across_y).start()
            else:
                for n in range(1, line):
                    out_copy(m, more_send[n - 1], {"row": (z + n) % line}).start()

        if square:
            f = m - 1

            @pl.when(within(f) & is_x)
            def _():
                out_copy(f, a_send, across_y).wait_recv()

                @pl.when(f % 2 == 0)
                def _():
                    out_copy(f, a_send, across_y).start()

            @pl.when(within(f) & is_y)
            def _():
                out_copy(f, a_send, across_x).wait_recv()

                @pl.when(f % 2 == 1)
                def _():
                    out_copy(f, a_send, across_x).start()

        return carry

    lax.fori_loop(0, CHUNKS + line, step, 0)

    def finish(i, carry):
        @pl.when(jnp.logical_not(is_root))
        def _():
            up_copy(i).wait_send()

        if square:
            @pl.when(is_root)
            def _():
                out_copy(i, a_send, across_x).wait_send()
                out_copy(i, b_send, across_y).wait_send()

            @pl.when((is_x & (i % 2 == 0)) | (is_y & (i % 2 == 1)))
            def _():
                out_copy(i, a_send, across_y).wait_send()

            @pl.when(is_far)
            def _():
                out_copy(i, a_send, across_y).wait_recv()
        else:
            @pl.when(is_root)
            def _():
                for n in range(1, line):
                    out_copy(i, more_send[n - 1], {"row": (z + n) % line}).wait_send()

            @pl.when(jnp.logical_not(is_root))
            def _():
                out_copy(i, more_send[0], {"row": z}).wait_recv()

        return carry

    lax.fori_loop(0, CHUNKS, finish, 0)


def collect(p, line):
    rows, cols = p.shape
    half = rows // 2
    chunk = half // CHUNKS
    buffer = pltpu.VMEM((half, cols), jnp.float32)
    extra = 0 if line == 4 else line - 1
    return pl.pallas_call(
        functools.partial(collect_kernel, line, chunk),
        out_shape=jax.ShapeDtypeStruct((half, cols), jnp.float32),
        in_specs=[pl.BlockSpec(memory_space=pltpu.VMEM)],
        out_specs=pl.BlockSpec(memory_space=pltpu.VMEM),
        scratch_shapes=[buffer] * 3
        + [pltpu.SemaphoreType.DMA] * 2
        + [pltpu.SemaphoreType.DMA((CHUNKS,))] * (6 + extra),
        compiler_params=pltpu.CompilerParams(
            collective_id=2, has_side_effects=True, vmem_limit_bytes=VMEM_LIMIT
        ),
        cost_estimate=pl.CostEstimate(flops=0, bytes_accessed=160 * 1000000, transcendentals=0),
        name="collect_product",
    )(p)


def product(a, b, dims):
    return lax.dot_general(
        a, b, (dims, ((), ())), precision=lax.Precision.HIGH, preferred_element_type=jnp.float32
    )


def identity_rows(first, count, start, width):
    rows_global = first + jnp.arange(count, dtype=jnp.int32)
    return (rows_global[:, None] == start + jnp.arange(width, dtype=jnp.int32)[None, :]).astype(
        jnp.float32
    )


def per_device(matrix, factor_inverse, panel, split_index):
    cols_loc = matrix.shape[1]
    width = factor_inverse.shape[0]
    ncol = lax.axis_size("col")
    line = lax.axis_size("row")
    assert ncol == 2 * line
    order = cols_loc * ncol
    col_idx = lax.axis_index("col")
    start = panel[0] * width
    owner = start // cols_loc
    offset = start - owner * cols_loc
    group = width // GROUPS

    partials, grams, collected = [], [], []
    for g in range(GROUPS):
        piece = lax.dynamic_slice_in_dim(matrix, offset + g * group, group, 1)
        piece = jnp.where(owner == col_idx, piece, jnp.float32(0.0))
        if partials:
            piece, partials[-1] = lax.optimization_barrier((piece, partials[-1]))
        columns = spread(piece, line)
        partials.append(product(matrix, columns, ((0,), (0,))))
    for g in range(GROUPS):
        if grams:
            partials[g], grams[-1] = lax.optimization_barrier((partials[g], grams[-1]))
        grams.append(
            lax.psum(partials[g], "row") / order
            + identity_rows(col_idx * cols_loc, cols_loc, start + g * group, group)
        )
    for g in range(GROUPS):
        collected.append(collect(product(matrix, grams[g], ((1,), (0,))), line))
    total = product(jnp.concatenate(collected, axis=1), factor_inverse, ((1,), (1,)))
    col_rows = order // ncol
    projector = 0.5 * (identity_rows(col_idx * col_rows, col_rows, start, width) + total)
    rows_global = col_idx * col_rows + jnp.arange(col_rows, dtype=jnp.int32)
    keep = (rows_global < order // 2) == (rows_global < split_index[0])
    return jnp.where(keep[:, None], projector, jnp.float32(0.0))


def solution(mesh):
    placed = (P("row", "col"), P(), P(), P())
    return jax.shard_map(
        per_device, mesh=mesh, in_specs=placed, out_specs=P("col", None), check_vma=False
    )
```

```python
import functools

import jax
import jax.numpy as jnp
from jax import lax
from jax.experimental import pallas as pl
from jax.experimental.pallas import tpu as pltpu
from jax.sharding import PartitionSpec as P

GROUPS = 2
CHUNKS = 32
SKEW = 3
VMEM_LIMIT = 40 * 1024 * 1024


def remote(src, dst, send, recv, target):
    return pltpu.make_async_remote_copy(
        src_ref=src,
        dst_ref=dst,
        send_sem=send,
        recv_sem=recv,
        device_id=target,
        device_id_type=pl.DeviceIdType.MESH,
    )


def signal(barrier, target):
    pl.semaphore_signal(barrier, inc=1, device_id=target, device_id_type=pl.DeviceIdType.MESH)


def spread_kernel(
    line, chunk, x_ref, o_ref, ex, rin, lin,
    ex_send, ex_recv, r_send, r_recv, l_send, l_recv, s_send, s_recv,
):
    c = lax.axis_index("col")
    z = c // 2
    k = c % 2
    half = CHUNKS * chunk
    base = pl.multiple_of(k * half, half)
    other = pl.multiple_of((1 - k) * half, half)
    sibling, up, down = {"col": c + 1 - 2 * k}, {"col": c + 2}, {"col": c - 2}
    has_down, has_up = z > 0, z < line - 1

    barrier = pltpu.get_barrier_semaphore()
    signal(barrier, sibling)

    @pl.when(has_down)
    def _():
        signal(barrier, down)

    @pl.when(has_up)
    def _():
        signal(barrier, up)

    pl.semaphore_wait(barrier, 1 + has_down.astype(jnp.int32) + has_up.astype(jnp.int32))

    swap = remote(x_ref.at[pl.ds(other, half)], ex, ex_send, ex_recv, sibling)
    swap.start()
    swap.wait()

    def rows_of(i):
        return pl.ds(pl.multiple_of(i * chunk, chunk), chunk)

    def whole_rows(i):
        return pl.ds(pl.multiple_of(base + i * chunk, chunk), chunk)

    def up_copy(i):
        return remote(rin.at[rows_of(i)], rin.at[rows_of(i)], r_send.at[i], r_recv.at[i], up)

    def down_copy(i):
        return remote(lin.at[rows_of(i)], lin.at[rows_of(i)], l_send.at[i], l_recv.at[i], down)

    def side_copy(i):
        return remote(
            o_ref.at[whole_rows(i)], o_ref.at[whole_rows(i)], s_send.at[i], s_recv.at[i], sibling
        )

    def own(i):
        return x_ref[whole_rows(i), :] + ex[rows_of(i), :]

    last = jnp.maximum(z, line - 1 - z)

    def step(t, carry):
        i = t - SKEW * z

        @pl.when((i >= 0) & (i < CHUNKS))
        def _():
            @pl.when(z == 0)
            def _():
                rin[rows_of(i), :] = own(i)

            @pl.when(has_down)
            def _():
                up_copy(i).wait_recv()
                rin[rows_of(i), :] = rin[rows_of(i), :] + own(i)

            @pl.when(has_up)
            def _():
                up_copy(i).start()

        j = t - SKEW * (line - 1 - z)

        @pl.when((j >= 0) & (j < CHUNKS))
        def _():
            @pl.when(z == line - 1)
            def _():
                lin[rows_of(j), :] = own(j)

            @pl.when(has_up)
            def _():
                down_copy(j).wait_recv()
                lin[rows_of(j), :] = lin[rows_of(j), :] + own(j)

            @pl.when(has_down)
            def _():
                down_copy(j).start()

        m = t - SKEW * last

        @pl.when((m >= 0) & (m < CHUNKS))
        def _():
            o_ref[whole_rows(m), :] = (rin[rows_of(m), :] + lin[rows_of(m), :]) - own(m)
            side_copy(m).start()

        return carry

    lax.fori_loop(0, CHUNKS + SKEW * (line - 1), step, 0)

    def finish(i, carry):
        @pl.when(has_up)
        def _():
            up_copy(i).wait_send()

        @pl.when(has_down)
        def _():
            down_copy(i).wait_send()

        side_copy(i).wait_send()
        remote(
            o_ref.at[pl.ds(pl.multiple_of(other + i * chunk, chunk), chunk)],
            o_ref.at[pl.ds(pl.multiple_of(other + i * chunk, chunk), chunk)],
            s_send.at[i], s_recv.at[i], sibling,
        ).wait_recv()
        return carry

    lax.fori_loop(0, CHUNKS, finish, 0)


def spread(x, line):
    rows, cols = x.shape
    half = rows // 2
    chunk = half // CHUNKS
    buffer = pltpu.VMEM((half, cols), jnp.float32)
    return pl.pallas_call(
        functools.partial(spread_kernel, line, chunk),
        out_shape=jax.ShapeDtypeStruct((rows, cols), jnp.float32),
        in_specs=[pl.BlockSpec(memory_space=pltpu.VMEM)],
        out_specs=pl.BlockSpec(memory_space=pltpu.VMEM),
        scratch_shapes=[buffer] * 3
        + [pltpu.SemaphoreType.DMA] * 2
        + [pltpu.SemaphoreType.DMA((CHUNKS,))] * 6,
        compiler_params=pltpu.CompilerParams(
            collective_id=1, has_side_effects=True, vmem_limit_bytes=VMEM_LIMIT
        ),
        cost_estimate=pl.CostEstimate(flops=0, bytes_accessed=160 * 1000000, transcendentals=0),
        name="spread_panel",
    )(x)


def collect_kernel(
    line, chunk, p_ref, o_ref, ex, rin, lin,
    ex_send, ex_recv, z_send, r_recv, l_recv, a_send, b_send, o_recv, *more_send,
):
    r = lax.axis_index("row")
    c = lax.axis_index("col")
    z = c // 2
    k = c % 2
    half = CHUNKS * chunk
    base = pl.multiple_of(k * half, half)
    other = pl.multiple_of((1 - k) * half, half)
    sibling, up, down = {"col": c + 1 - 2 * k}, {"col": c + 2}, {"col": c - 2}
    square = line == 4
    is_root = r == z
    if square:
        across_x, across_y = {"row": r + 1 - 2 * (r % 2)}, {"row": r + 2 - 4 * (r // 2)}
        same_x, same_y = (r % 2) == (z % 2), (r // 2) == (z // 2)
        is_x = jnp.logical_not(same_x) & same_y
        is_y = same_x & jnp.logical_not(same_y)
        is_far = jnp.logical_not(same_x) & jnp.logical_not(same_y)

    barrier = pltpu.get_barrier_semaphore()
    signal(barrier, sibling)

    @pl.when((z > 0) & (z <= r))
    def _():
        signal(barrier, down)

    @pl.when((z < line - 1) & (z >= r))
    def _():
        signal(barrier, up)

    if square:
        @pl.when(is_x | is_far)
        def _():
            signal(barrier, across_x)

        @pl.when(is_y | is_far)
        def _():
            signal(barrier, across_y)
    else:
        @pl.when(jnp.logical_not(is_root))
        def _():
            signal(barrier, {"row": z})

    if square:
        pl.semaphore_wait(barrier, jnp.where(is_far, 2, 3))
    else:
        pl.semaphore_wait(barrier, jnp.where(is_root, line, 2))

    swap = remote(p_ref.at[pl.ds(other, half)], ex, ex_send, ex_recv, sibling)
    swap.start()
    swap.wait()

    def rows_of(i):
        return pl.ds(pl.multiple_of(i * chunk, chunk), chunk)

    def own(i):
        return p_ref[pl.ds(pl.multiple_of(base + i * chunk, chunk), chunk), :] + ex[rows_of(i), :]

    def up_copy(i):
        return remote(rin.at[rows_of(i)], rin.at[rows_of(i)], z_send.at[i], r_recv.at[i], up)

    def down_copy(i):
        return remote(lin.at[rows_of(i)], lin.at[rows_of(i)], z_send.at[i], l_recv.at[i], down)

    def out_copy(i, sems, target):
        return remote(o_ref.at[rows_of(i)], o_ref.at[rows_of(i)], sems.at[i], o_recv.at[i], target)

    last = jnp.maximum(z, line - 1 - z)

    def within(i):
        return (i >= 0) & (i < CHUNKS)

    def step(t, carry):
        i = t - SKEW * z

        @pl.when(within(i) & (z < r))
        def _():
            @pl.when(z == 0)
            def _():
                rin[rows_of(i), :] = own(i)

            @pl.when(z > 0)
            def _():
                up_copy(i).wait_recv()
                rin[rows_of(i), :] = rin[rows_of(i), :] + own(i)

            up_copy(i).start()

        j = t - SKEW * (line - 1 - z)

        @pl.when(within(j) & (z > r))
        def _():
            @pl.when(z == line - 1)
            def _():
                lin[rows_of(j), :] = own(j)

            @pl.when(z < line - 1)
            def _():
                down_copy(j).wait_recv()
                lin[rows_of(j), :] = lin[rows_of(j), :] + own(j)

            down_copy(j).start()

        m = t - SKEW * last

        @pl.when(within(m) & is_root)
        def _():
            o_ref[rows_of(m), :] = own(m)

            @pl.when(z > 0)
            def _():
                up_copy(m).wait_recv()
                o_ref[rows_of(m), :] = o_ref[rows_of(m), :] + rin[rows_of(m), :]

            @pl.when(z < line - 1)
            def _():
                down_copy(m).wait_recv()
                o_ref[rows_of(m), :] = o_ref[rows_of(m), :] + lin[rows_of(m), :]

            if square:
                out_copy(m, a_send, across_x).start()
                out_copy(m, b_send, across_y).start()
            else:
                for n in range(1, line):
                    out_copy(m, more_send[n - 1], {"row": (z + n) % line}).start()

        if square:
            f = m - SKEW

            @pl.when(within(f) & is_x)
            def _():
                out_copy(f, a_send, across_y).wait_recv()

                @pl.when(f % 2 == 0)
                def _():
                    out_copy(f, a_send, across_y).start()

            @pl.when(within(f) & is_y)
            def _():
                out_copy(f, a_send, across_x).wait_recv()

                @pl.when(f % 2 == 1)
                def _():
                    out_copy(f, a_send, across_x).start()

        return carry

    lax.fori_loop(0, CHUNKS + SKEW * line, step, 0)

    def finish(i, carry):
        @pl.when(jnp.logical_not(is_root))
        def _():
            up_copy(i).wait_send()

        if square:
            @pl.when(is_root)
            def _():
                out_copy(i, a_send, across_x).wait_send()
                out_copy(i, b_send, across_y).wait_send()

            @pl.when((is_x & (i % 2 == 0)) | (is_y & (i % 2 == 1)))
            def _():
                out_copy(i, a_send, across_y).wait_send()

            @pl.when(is_far)
            def _():
                out_copy(i, a_send, across_y).wait_recv()
        else:
            @pl.when(is_root)
            def _():
                for n in range(1, line):
                    out_copy(i, more_send[n - 1], {"row": (z + n) % line}).wait_send()

            @pl.when(jnp.logical_not(is_root))
            def _():
                out_copy(i, more_send[0], {"row": z}).wait_recv()

        return carry

    lax.fori_loop(0, CHUNKS, finish, 0)


def collect(p, line):
    rows, cols = p.shape
    half = rows // 2
    chunk = half // CHUNKS
    buffer = pltpu.VMEM((half, cols), jnp.float32)
    extra = 0 if line == 4 else line - 1
    return pl.pallas_call(
        functools.partial(collect_kernel, line, chunk),
        out_shape=jax.ShapeDtypeStruct((half, cols), jnp.float32),
        in_specs=[pl.BlockSpec(memory_space=pltpu.VMEM)],
        out_specs=pl.BlockSpec(memory_space=pltpu.VMEM),
        scratch_shapes=[buffer] * 3
        + [pltpu.SemaphoreType.DMA] * 2
        + [pltpu.SemaphoreType.DMA((CHUNKS,))] * (6 + extra),
        compiler_params=pltpu.CompilerParams(
            collective_id=2, has_side_effects=True, vmem_limit_bytes=VMEM_LIMIT
        ),
        cost_estimate=pl.CostEstimate(flops=0, bytes_accessed=160 * 1000000, transcendentals=0),
        name="collect_product",
    )(p)


def product(a, b, dims):
    return lax.dot_general(
        a, b, (dims, ((), ())), precision=lax.Precision.HIGH, preferred_element_type=jnp.float32
    )


def identity_rows(first, count, start, width):
    rows_global = first + jnp.arange(count, dtype=jnp.int32)
    return (rows_global[:, None] == start + jnp.arange(width, dtype=jnp.int32)[None, :]).astype(
        jnp.float32
    )


def per_device(matrix, factor_inverse, panel, split_index):
    cols_loc = matrix.shape[1]
    width = factor_inverse.shape[0]
    ncol = lax.axis_size("col")
    line = lax.axis_size("row")
    assert ncol == 2 * line
    order = cols_loc * ncol
    col_idx = lax.axis_index("col")
    start = panel[0] * width
    owner = start // cols_loc
    offset = start - owner * cols_loc
    group = width // GROUPS

    partials, grams, collected = [], [], []
    for g in range(GROUPS):
        piece = lax.dynamic_slice_in_dim(matrix, offset + g * group, group, 1)
        piece = jnp.where(owner == col_idx, piece, jnp.float32(0.0))
        if partials:
            piece, partials[-1] = lax.optimization_barrier((piece, partials[-1]))
        columns = spread(piece, line)
        partials.append(product(matrix, columns, ((0,), (0,))))
    for g in range(GROUPS):
        if grams:
            partials[g], grams[-1] = lax.optimization_barrier((partials[g], grams[-1]))
        grams.append(
            lax.psum(partials[g], "row") / order
            + identity_rows(col_idx * cols_loc, cols_loc, start + g * group, group)
        )
    for g in range(GROUPS):
        collected.append(collect(product(matrix, grams[g], ((1,), (0,))), line))
    total = product(jnp.concatenate(collected, axis=1), factor_inverse, ((1,), (1,)))
    col_rows = order // ncol
    projector = 0.5 * (identity_rows(col_idx * col_rows, col_rows, start, width) + total)
    rows_global = col_idx * col_rows + jnp.arange(col_rows, dtype=jnp.int32)
    keep = (rows_global < order // 2) == (rows_global < split_index[0])
    return jnp.where(keep[:, None], projector, jnp.float32(0.0))


def solution(mesh):
    placed = (P("row", "col"), P(), P(), P())
    return jax.shard_map(
        per_device, mesh=mesh, in_specs=placed, out_specs=P("col", None), check_vma=False
    )
```

```python
import functools

import jax
import jax.numpy as jnp
from jax import lax
from jax.experimental import pallas as pl
from jax.experimental.pallas import tpu as pltpu
from jax.sharding import PartitionSpec as P

GROUPS = 2
CHUNKS = 32
SKEW = 3
BLOCKS = 4
EACH = CHUNKS // BLOCKS
VMEM_LIMIT = 40 * 1024 * 1024


def remote(src, dst, send, recv, target):
    return pltpu.make_async_remote_copy(
        src_ref=src,
        dst_ref=dst,
        send_sem=send,
        recv_sem=recv,
        device_id=target,
        device_id_type=pl.DeviceIdType.MESH,
    )


def signal(barrier, target):
    pl.semaphore_signal(barrier, inc=1, device_id=target, device_id_type=pl.DeviceIdType.MESH)


def parts_of(x):
    high = x.astype(jnp.bfloat16)
    return high, (x - high.astype(jnp.float32)).astype(jnp.bfloat16)


def split_dot(a, b):
    total = jnp.dot(a[1], b[0], preferred_element_type=jnp.float32)
    total = total + jnp.dot(a[0], b[1], preferred_element_type=jnp.float32)
    return total + jnp.dot(a[0], b[0], preferred_element_type=jnp.float32)


def spread_kernel(
    line, chunk, x_ref, a_ref, g_ref, o_ref, a_buf, a_sem, ex, rin, lin,
    ex_send, ex_recv, r_send, r_recv, l_send, l_recv, s_send, s_recv,
):
    c = lax.axis_index("col")
    z = c // 2
    k = c % 2
    half = CHUNKS * chunk
    base = pl.multiple_of(k * half, half)
    other = pl.multiple_of((1 - k) * half, half)
    sibling, up, down = {"col": c + 1 - 2 * k}, {"col": c + 2}, {"col": c - 2}
    has_down, has_up = z > 0, z < line - 1

    barrier = pltpu.get_barrier_semaphore()
    signal(barrier, sibling)

    @pl.when(has_down)
    def _():
        signal(barrier, down)

    @pl.when(has_up)
    def _():
        signal(barrier, up)

    pl.semaphore_wait(barrier, 1 + has_down.astype(jnp.int32) + has_up.astype(jnp.int32))

    block = EACH * chunk

    def block_rows(q):
        half_no = (k + q) % 2
        return pl.ds(pl.multiple_of(half_no * half + (q // 2) * block, block), block)

    def load(q):
        slot = q % 2
        return pltpu.make_async_copy(a_ref.at[block_rows(q)], a_buf.at[slot], a_sem.at[slot])

    load(0).start()
    load(1).start()
    g_ref[...] = jnp.zeros_like(g_ref)

    def accumulate(q):
        load(q).wait()
        panel = parts_of(jnp.transpose(o_ref[block_rows(q), :]))
        g_ref[...] += split_dot(panel, parts_of(a_buf[q % 2]))

        @pl.when(q + 2 < 2 * BLOCKS)
        def _():
            load(q + 2).start()

    swap = remote(x_ref.at[pl.ds(other, half)], ex, ex_send, ex_recv, sibling)
    swap.start()
    swap.wait()

    def rows_of(i):
        return pl.ds(pl.multiple_of(i * chunk, chunk), chunk)

    def whole_rows(i):
        return pl.ds(pl.multiple_of(base + i * chunk, chunk), chunk)

    def up_copy(i):
        return remote(rin.at[rows_of(i)], rin.at[rows_of(i)], r_send.at[i], r_recv.at[i], up)

    def down_copy(i):
        return remote(lin.at[rows_of(i)], lin.at[rows_of(i)], l_send.at[i], l_recv.at[i], down)

    def side_copy(i):
        return remote(
            o_ref.at[whole_rows(i)], o_ref.at[whole_rows(i)], s_send.at[i], s_recv.at[i], sibling
        )

    def side_wait(i):
        rows = pl.ds(pl.multiple_of(other + i * chunk, chunk), chunk)
        remote(o_ref.at[rows], o_ref.at[rows], s_send.at[i], s_recv.at[i], sibling).wait_recv()

    def accumulate_side(b):
        def wait_one(n, carry):
            side_wait(b * EACH + n)
            return carry

        lax.fori_loop(0, EACH, wait_one, 0)
        accumulate(2 * b + 1)

    def own(i):
        return x_ref[whole_rows(i), :] + ex[rows_of(i), :]

    last = jnp.maximum(z, line - 1 - z)

    def step(t, carry):
        i = t - SKEW * z

        @pl.when((i >= 0) & (i < CHUNKS))
        def _():
            @pl.when(z == 0)
            def _():
                rin[rows_of(i), :] = own(i)

            @pl.when(has_down)
            def _():
                up_copy(i).wait_recv()
                rin[rows_of(i), :] = rin[rows_of(i), :] + own(i)

            @pl.when(has_up)
            def _():
                up_copy(i).start()

        j = t - SKEW * (line - 1 - z)

        @pl.when((j >= 0) & (j < CHUNKS))
        def _():
            @pl.when(z == line - 1)
            def _():
                lin[rows_of(j), :] = own(j)

            @pl.when(has_up)
            def _():
                down_copy(j).wait_recv()
                lin[rows_of(j), :] = lin[rows_of(j), :] + own(j)

            @pl.when(has_down)
            def _():
                down_copy(j).start()

        m = t - SKEW * last

        @pl.when((m >= 0) & (m < CHUNKS))
        def _():
            o_ref[whole_rows(m), :] = (rin[rows_of(m), :] + lin[rows_of(m), :]) - own(m)
            side_copy(m).start()

            @pl.when(m % EACH == EACH - 1)
            def _():
                accumulate(2 * (m // EACH))

            @pl.when((m % EACH == EACH // 2 - 1) & (m >= EACH))
            def _():
                accumulate_side(m // EACH - 1)

        return carry

    lax.fori_loop(0, CHUNKS + SKEW * (line - 1), step, 0)

    accumulate_side(BLOCKS - 1)

    def finish(i, carry):
        @pl.when(has_up)
        def _():
            up_copy(i).wait_send()

        @pl.when(has_down)
        def _():
            down_copy(i).wait_send()

        side_copy(i).wait_send()
        return carry

    lax.fori_loop(0, CHUNKS, finish, 0)


def spread(x, matrix, line):
    rows, cols = x.shape
    depth = matrix.shape[1]
    half = rows // 2
    chunk = half // CHUNKS
    buffer = pltpu.VMEM((half, cols), jnp.float32)
    return pl.pallas_call(
        functools.partial(spread_kernel, line, chunk),
        out_shape=jax.ShapeDtypeStruct((cols, depth), jnp.float32),
        in_specs=[pl.BlockSpec(memory_space=pltpu.VMEM), pl.BlockSpec(memory_space=pl.ANY)],
        out_specs=pl.BlockSpec(memory_space=pltpu.VMEM),
        scratch_shapes=[
            pltpu.VMEM((rows, cols), jnp.float32),
            pltpu.VMEM((2, EACH * chunk, depth), jnp.float32),
            pltpu.SemaphoreType.DMA((2,)),
        ]
        + [buffer] * 3
        + [pltpu.SemaphoreType.DMA] * 2
        + [pltpu.SemaphoreType.DMA((CHUNKS,))] * 6,
        compiler_params=pltpu.CompilerParams(
            collective_id=1, has_side_effects=True, vmem_limit_bytes=VMEM_LIMIT
        ),
        cost_estimate=pl.CostEstimate(
            flops=6 * rows * cols * depth, bytes_accessed=220 * 1000000, transcendentals=0
        ),
        name="spread_panel",
    )(x, matrix)


def collect_kernel(
    line, chunk, g_ref, a_ref, o_ref, a_buf, a_sem, g_high, g_low, p_own, p_other, ex, rin, lin,
    ex_send, ex_recv, z_send, r_recv, l_recv, a_send, b_send, o_recv, *more_send,
):
    r = lax.axis_index("row")
    c = lax.axis_index("col")
    z = c // 2
    k = c % 2
    half = CHUNKS * chunk
    base = pl.multiple_of(k * half, half)
    other = pl.multiple_of((1 - k) * half, half)
    sibling, up, down = {"col": c + 1 - 2 * k}, {"col": c + 2}, {"col": c - 2}
    square = line == 4
    is_root = r == z
    if square:
        across_x, across_y = {"row": r + 1 - 2 * (r % 2)}, {"row": r + 2 - 4 * (r // 2)}
        same_x, same_y = (r % 2) == (z % 2), (r // 2) == (z // 2)
        is_x = jnp.logical_not(same_x) & same_y
        is_y = same_x & jnp.logical_not(same_y)
        is_far = jnp.logical_not(same_x) & jnp.logical_not(same_y)

    barrier = pltpu.get_barrier_semaphore()
    signal(barrier, sibling)

    @pl.when((z > 0) & (z <= r))
    def _():
        signal(barrier, down)

    @pl.when((z < line - 1) & (z >= r))
    def _():
        signal(barrier, up)

    if square:
        @pl.when(is_x | is_far)
        def _():
            signal(barrier, across_x)

        @pl.when(is_y | is_far)
        def _():
            signal(barrier, across_y)
    else:
        @pl.when(jnp.logical_not(is_root))
        def _():
            signal(barrier, {"row": z})

    if square:
        pl.semaphore_wait(barrier, jnp.where(is_far, 2, 3))
    else:
        pl.semaphore_wait(barrier, jnp.where(is_root, line, 2))

    block = EACH * chunk

    def load(q):
        slot = q % 2
        first = ((1 - k + q) % 2) * half + (q // 2) * block
        rows = pl.ds(pl.multiple_of(first, block), block)
        return pltpu.make_async_copy(a_ref.at[rows], a_buf.at[slot], a_sem.at[slot])

    def block_rows(b):
        return pl.ds(pl.multiple_of(b * block, block), block)

    def multiply(q, target):
        load(q).wait()
        target[block_rows(q // 2), :] = split_dot(
            parts_of(a_buf[q % 2]), (g_high[...], g_low[...])
        )

        @pl.when(q + 2 < 2 * BLOCKS)
        def _():
            load(q + 2).start()

    def swap(b):
        rows = block_rows(b)
        return remote(p_other.at[rows], ex.at[rows], ex_send.at[b], ex_recv.at[b], sibling)

    load(0).start()
    load(1).start()
    g_high[...], g_low[...] = parts_of(g_ref[...])
    multiply(0, p_other)
    swap(0).start()
    multiply(1, p_own)

    def rows_of(i):
        return pl.ds(pl.multiple_of(i * chunk, chunk), chunk)

    def own(i):
        return p_own[rows_of(i), :] + ex[rows_of(i), :]

    def up_copy(i):
        return remote(rin.at[rows_of(i)], rin.at[rows_of(i)], z_send.at[i], r_recv.at[i], up)

    def down_copy(i):
        return remote(lin.at[rows_of(i)], lin.at[rows_of(i)], z_send.at[i], l_recv.at[i], down)

    def out_copy(i, sems, target):
        return remote(o_ref.at[rows_of(i)], o_ref.at[rows_of(i)], sems.at[i], o_recv.at[i], target)

    last = jnp.maximum(z, line - 1 - z)

    def within(i):
        return (i >= 0) & (i < CHUNKS)

    def step(t, carry):
        now = t // EACH

        @pl.when((t % EACH == 0) & (now < BLOCKS))
        def _():
            swap(now).wait_recv()

        @pl.when((t % EACH == 0) & (now < BLOCKS - 1))
        def _():
            multiply(2 * now + 2, p_other)
            swap(now + 1).start()

        @pl.when((t % EACH == EACH // 2) & (now < BLOCKS - 1))
        def _():
            multiply(2 * now + 3, p_own)

        i = t - SKEW * z

        @pl.when(within(i) & (z < r))
        def _():
            @pl.when(z == 0)
            def _():
                rin[rows_of(i), :] = own(i)

            @pl.when(z > 0)
            def _():
                up_copy(i).wait_recv()
                rin[rows_of(i), :] = rin[rows_of(i), :] + own(i)

            up_copy(i).start()

        j = t - SKEW * (line - 1 - z)

        @pl.when(within(j) & (z > r))
        def _():
            @pl.when(z == line - 1)
            def _():
                lin[rows_of(j), :] = own(j)

            @pl.when(z < line - 1)
            def _():
                down_copy(j).wait_recv()
                lin[rows_of(j), :] = lin[rows_of(j), :] + own(j)

            down_copy(j).start()

        m = t - SKEW * last

        @pl.when(within(m) & is_root)
        def _():
            o_ref[rows_of(m), :] = own(m)

            @pl.when(z > 0)
            def _():
                up_copy(m).wait_recv()
                o_ref[rows_of(m), :] = o_ref[rows_of(m), :] + rin[rows_of(m), :]

            @pl.when(z < line - 1)
            def _():
                down_copy(m).wait_recv()
                o_ref[rows_of(m), :] = o_ref[rows_of(m), :] + lin[rows_of(m), :]

            if square:
                out_copy(m, a_send, across_x).start()
                out_copy(m, b_send, across_y).start()
            else:
                for n in range(1, line):
                    out_copy(m, more_send[n - 1], {"row": (z + n) % line}).start()

        if square:
            f = m - SKEW

            @pl.when(within(f) & is_x)
            def _():
                out_copy(f, a_send, across_y).wait_recv()

                @pl.when(f % 2 == 0)
                def _():
                    out_copy(f, a_send, across_y).start()

            @pl.when(within(f) & is_y)
            def _():
                out_copy(f, a_send, across_x).wait_recv()

                @pl.when(f % 2 == 1)
                def _():
                    out_copy(f, a_send, across_x).start()

        return carry

    lax.fori_loop(0, CHUNKS + SKEW * line, step, 0)

    for b in range(BLOCKS):
        swap(b).wait_send()

    def finish(i, carry):
        @pl.when(jnp.logical_not(is_root))
        def _():
            up_copy(i).wait_send()

        if square:
            @pl.when(is_root)
            def _():
                out_copy(i, a_send, across_x).wait_send()
                out_copy(i, b_send, across_y).wait_send()

            @pl.when((is_x & (i % 2 == 0)) | (is_y & (i % 2 == 1)))
            def _():
                out_copy(i, a_send, across_y).wait_send()

            @pl.when(is_far)
            def _():
                out_copy(i, a_send, across_y).wait_recv()
        else:
            @pl.when(is_root)
            def _():
                for n in range(1, line):
                    out_copy(i, more_send[n - 1], {"row": (z + n) % line}).wait_send()

            @pl.when(jnp.logical_not(is_root))
            def _():
                out_copy(i, more_send[0], {"row": z}).wait_recv()

        return carry

    lax.fori_loop(0, CHUNKS, finish, 0)


def collect(gram, matrix, line):
    depth, cols = gram.shape
    half = matrix.shape[0] // 2
    chunk = half // CHUNKS
    buffer = pltpu.VMEM((half, cols), jnp.float32)
    extra = 0 if line == 4 else line - 1
    return pl.pallas_call(
        functools.partial(collect_kernel, line, chunk),
        out_shape=jax.ShapeDtypeStruct((half, cols), jnp.float32),
        in_specs=[pl.BlockSpec(memory_space=pltpu.VMEM), pl.BlockSpec(memory_space=pl.ANY)],
        out_specs=pl.BlockSpec(memory_space=pltpu.VMEM),
        scratch_shapes=[
            pltpu.VMEM((2, EACH * chunk, depth), jnp.float32),
            pltpu.SemaphoreType.DMA((2,)),
        ]
        + [pltpu.VMEM((depth, cols), jnp.bfloat16)] * 2
        + [buffer] * 5
        + [pltpu.SemaphoreType.DMA((BLOCKS,))] * 2
        + [pltpu.SemaphoreType.DMA((CHUNKS,))] * (6 + extra),
        compiler_params=pltpu.CompilerParams(
            collective_id=2, has_side_effects=True, vmem_limit_bytes=VMEM_LIMIT
        ),
        cost_estimate=pl.CostEstimate(
            flops=12 * half * cols * depth, bytes_accessed=220 * 1000000, transcendentals=0
        ),
        name="collect_product",
    )(gram, matrix)


def product(a, b, dims):
    return lax.dot_general(
        a, b, (dims, ((), ())), precision=lax.Precision.HIGH, preferred_element_type=jnp.float32
    )


def identity_rows(first, count, start, width):
    rows_global = first + jnp.arange(count, dtype=jnp.int32)
    return (rows_global[:, None] == start + jnp.arange(width, dtype=jnp.int32)[None, :]).astype(
        jnp.float32
    )


def per_device(matrix, factor_inverse, panel, split_index):
    cols_loc = matrix.shape[1]
    width = factor_inverse.shape[0]
    ncol = lax.axis_size("col")
    line = lax.axis_size("row")
    assert ncol == 2 * line
    order = cols_loc * ncol
    col_idx = lax.axis_index("col")
    start = panel[0] * width
    owner = start // cols_loc
    offset = start - owner * cols_loc
    group = width // GROUPS

    partials, grams, collected = [], [], []
    for g in range(GROUPS):
        piece = lax.dynamic_slice_in_dim(matrix, offset + g * group, group, 1)
        piece = jnp.where(owner == col_idx, piece, jnp.float32(0.0))
        if partials:
            piece, partials[-1] = lax.optimization_barrier((piece, partials[-1]))
        partials.append(spread(piece, matrix, line))
    for g in range(GROUPS):
        if grams:
            partials[g], grams[-1] = lax.optimization_barrier((partials[g], grams[-1]))
        grams.append(
            lax.psum(partials[g], "row").T / order
            + identity_rows(col_idx * cols_loc, cols_loc, start + g * group, group)
        )
    for g in range(GROUPS):
        collected.append(collect(grams[g], matrix, line))
    total = product(jnp.concatenate(collected, axis=1), factor_inverse, ((1,), (1,)))
    col_rows = order // ncol
    projector = 0.5 * (identity_rows(col_idx * col_rows, col_rows, start, width) + total)
    rows_global = col_idx * col_rows + jnp.arange(col_rows, dtype=jnp.int32)
    keep = (rows_global < order // 2) == (rows_global < split_index[0])
    return jnp.where(keep[:, None], projector, jnp.float32(0.0))


def solution(mesh):
    placed = (P("row", "col"), P(), P(), P())
    return jax.shard_map(
        per_device, mesh=mesh, in_specs=placed, out_specs=P("col", None), check_vma=False
    )
```

```python
import functools

import jax
import jax.numpy as jnp
from jax import lax
from jax.experimental import pallas as pl
from jax.experimental.pallas import tpu as pltpu
from jax.sharding import PartitionSpec as P

GROUPS = 2
CHUNKS = 32
SKEW = 3
BLOCKS = 8
EACH = CHUNKS // BLOCKS
VMEM_LIMIT = 40 * 1024 * 1024


def remote(src, dst, send, recv, target):
    return pltpu.make_async_remote_copy(
        src_ref=src,
        dst_ref=dst,
        send_sem=send,
        recv_sem=recv,
        device_id=target,
        device_id_type=pl.DeviceIdType.MESH,
    )


def signal(barrier, target):
    pl.semaphore_signal(barrier, inc=1, device_id=target, device_id_type=pl.DeviceIdType.MESH)


def parts_of(x):
    high = x.astype(jnp.bfloat16)
    return high, (x - high.astype(jnp.float32)).astype(jnp.bfloat16)


def split_dot(a, b):
    total = jnp.dot(a[1], b[0], preferred_element_type=jnp.float32)
    total = total + jnp.dot(a[0], b[1], preferred_element_type=jnp.float32)
    return total + jnp.dot(a[0], b[0], preferred_element_type=jnp.float32)


def spread_kernel(
    line, chunk, x_ref, a_ref, g_ref, o_ref, a_buf, a_sem, ex, rin, lin,
    ex_send, ex_recv, r_send, r_recv, l_send, l_recv, s_send, s_recv,
):
    c = lax.axis_index("col")
    z = c // 2
    k = c % 2
    half = CHUNKS * chunk
    base = pl.multiple_of(k * half, half)
    other = pl.multiple_of((1 - k) * half, half)
    sibling, up, down = {"col": c + 1 - 2 * k}, {"col": c + 2}, {"col": c - 2}
    has_down, has_up = z > 0, z < line - 1

    barrier = pltpu.get_barrier_semaphore()
    signal(barrier, sibling)

    @pl.when(has_down)
    def _():
        signal(barrier, down)

    @pl.when(has_up)
    def _():
        signal(barrier, up)

    block = EACH * chunk

    def block_rows(q):
        half_no = (k + q) % 2
        return pl.ds(pl.multiple_of(half_no * half + (q // 2) * block, block), block)

    def load(q):
        slot = q % 2
        return pltpu.make_async_copy(a_ref.at[block_rows(q)], a_buf.at[slot], a_sem.at[slot])

    load(0).start()
    load(1).start()
    g_ref[...] = jnp.zeros_like(g_ref)

    pl.semaphore_wait(barrier, 1 + has_down.astype(jnp.int32) + has_up.astype(jnp.int32))

    def accumulate(q):
        load(q).wait()
        panel = parts_of(jnp.transpose(o_ref[block_rows(q), :]))
        g_ref[...] += split_dot(panel, parts_of(a_buf[q % 2]))

        @pl.when(q + 2 < 2 * BLOCKS)
        def _():
            load(q + 2).start()

    def swap(b):
        rows = pl.ds(pl.multiple_of(b * block, block), block)
        source = pl.ds(pl.multiple_of(other + b * block, block), block)
        return remote(x_ref.at[source], ex.at[rows], ex_send.at[b], ex_recv.at[b], sibling)

    for b in range(BLOCKS):
        swap(b).start()

    def rows_of(i):
        return pl.ds(pl.multiple_of(i * chunk, chunk), chunk)

    def whole_rows(i):
        return pl.ds(pl.multiple_of(base + i * chunk, chunk), chunk)

    def up_copy(i):
        return remote(rin.at[rows_of(i)], rin.at[rows_of(i)], r_send.at[i], r_recv.at[i], up)

    def down_copy(i):
        return remote(lin.at[rows_of(i)], lin.at[rows_of(i)], l_send.at[i], l_recv.at[i], down)

    def side_copy(i):
        return remote(
            o_ref.at[whole_rows(i)], o_ref.at[whole_rows(i)], s_send.at[i], s_recv.at[i], sibling
        )

    def side_wait(i):
        rows = pl.ds(pl.multiple_of(other + i * chunk, chunk), chunk)
        remote(o_ref.at[rows], o_ref.at[rows], s_send.at[i], s_recv.at[i], sibling).wait_recv()

    def accumulate_side(b):
        def wait_one(n, carry):
            side_wait(b * EACH + n)
            return carry

        lax.fori_loop(0, EACH, wait_one, 0)
        accumulate(2 * b + 1)

    def own(i):
        return x_ref[whole_rows(i), :] + ex[rows_of(i), :]

    last = jnp.maximum(z, line - 1 - z)

    def step(t, carry):
        @pl.when((t % EACH == 0) & (t < CHUNKS))
        def _():
            swap(t // EACH).wait_recv()

        i = t - SKEW * z

        @pl.when((i >= 0) & (i < CHUNKS))
        def _():
            @pl.when(z == 0)
            def _():
                rin[rows_of(i), :] = own(i)

            @pl.when(has_down)
            def _():
                up_copy(i).wait_recv()
                rin[rows_of(i), :] = rin[rows_of(i), :] + own(i)

            @pl.when(has_up)
            def _():
                up_copy(i).start()

        j = t - SKEW * (line - 1 - z)

        @pl.when((j >= 0) & (j < CHUNKS))
        def _():
            @pl.when(z == line - 1)
            def _():
                lin[rows_of(j), :] = own(j)

            @pl.when(has_up)
            def _():
                down_copy(j).wait_recv()
                lin[rows_of(j), :] = lin[rows_of(j), :] + own(j)

            @pl.when(has_down)
            def _():
                down_copy(j).start()

        m = t - SKEW * last

        @pl.when((m >= 0) & (m < CHUNKS))
        def _():
            o_ref[whole_rows(m), :] = (rin[rows_of(m), :] + lin[rows_of(m), :]) - own(m)
            side_copy(m).start()

            @pl.when(m % EACH == EACH - 1)
            def _():
                accumulate(2 * (m // EACH))

            @pl.when((m % EACH == EACH // 2 - 1) & (m >= EACH))
            def _():
                accumulate_side(m // EACH - 1)

        return carry

    lax.fori_loop(0, CHUNKS + SKEW * (line - 1), step, 0)

    accumulate_side(BLOCKS - 1)
    for b in range(BLOCKS):
        swap(b).wait_send()

    def finish(i, carry):
        @pl.when(has_up)
        def _():
            up_copy(i).wait_send()

        @pl.when(has_down)
        def _():
            down_copy(i).wait_send()

        side_copy(i).wait_send()
        return carry

    lax.fori_loop(0, CHUNKS, finish, 0)


def spread(x, matrix, line):
    rows, cols = x.shape
    depth = matrix.shape[1]
    half = rows // 2
    chunk = half // CHUNKS
    buffer = pltpu.VMEM((half, cols), jnp.float32)
    return pl.pallas_call(
        functools.partial(spread_kernel, line, chunk),
        out_shape=jax.ShapeDtypeStruct((cols, depth), jnp.float32),
        in_specs=[pl.BlockSpec(memory_space=pltpu.VMEM), pl.BlockSpec(memory_space=pl.ANY)],
        out_specs=pl.BlockSpec(memory_space=pltpu.VMEM),
        scratch_shapes=[
            pltpu.VMEM((rows, cols), jnp.float32),
            pltpu.VMEM((2, EACH * chunk, depth), jnp.float32),
            pltpu.SemaphoreType.DMA((2,)),
        ]
        + [buffer] * 3
        + [pltpu.SemaphoreType.DMA((BLOCKS,))] * 2
        + [pltpu.SemaphoreType.DMA((CHUNKS,))] * 6,
        compiler_params=pltpu.CompilerParams(
            collective_id=1, has_side_effects=True, vmem_limit_bytes=VMEM_LIMIT
        ),
        cost_estimate=pl.CostEstimate(
            flops=6 * rows * cols * depth, bytes_accessed=220 * 1000000, transcendentals=0
        ),
        name="spread_panel",
    )(x, matrix)


def collect_kernel(
    line, chunk, g_ref, a_ref, o_ref, a_buf, a_sem, g_high, g_low, p_own, p_other, ex, rin, lin,
    ex_send, ex_recv, z_send, r_recv, l_recv, a_send, b_send, o_recv, *more_send,
):
    r = lax.axis_index("row")
    c = lax.axis_index("col")
    z = c // 2
    k = c % 2
    half = CHUNKS * chunk
    base = pl.multiple_of(k * half, half)
    other = pl.multiple_of((1 - k) * half, half)
    sibling, up, down = {"col": c + 1 - 2 * k}, {"col": c + 2}, {"col": c - 2}
    square = line == 4
    is_root = r == z
    if square:
        across_x, across_y = {"row": r + 1 - 2 * (r % 2)}, {"row": r + 2 - 4 * (r // 2)}
        same_x, same_y = (r % 2) == (z % 2), (r // 2) == (z // 2)
        is_x = jnp.logical_not(same_x) & same_y
        is_y = same_x & jnp.logical_not(same_y)
        is_far = jnp.logical_not(same_x) & jnp.logical_not(same_y)

    barrier = pltpu.get_barrier_semaphore()
    signal(barrier, sibling)

    @pl.when((z > 0) & (z <= r))
    def _():
        signal(barrier, down)

    @pl.when((z < line - 1) & (z >= r))
    def _():
        signal(barrier, up)

    if square:
        @pl.when(is_x | is_far)
        def _():
            signal(barrier, across_x)

        @pl.when(is_y | is_far)
        def _():
            signal(barrier, across_y)
    else:
        @pl.when(jnp.logical_not(is_root))
        def _():
            signal(barrier, {"row": z})

    block = EACH * chunk

    def load(q):
        slot = q % 2
        first = ((1 - k + q) % 2) * half + (q // 2) * block
        rows = pl.ds(pl.multiple_of(first, block), block)
        return pltpu.make_async_copy(a_ref.at[rows], a_buf.at[slot], a_sem.at[slot])

    def block_rows(b):
        return pl.ds(pl.multiple_of(b * block, block), block)

    def multiply(q, target):
        load(q).wait()
        target[block_rows(q // 2), :] = split_dot(
            parts_of(a_buf[q % 2]), (g_high[...], g_low[...])
        )

        @pl.when(q + 2 < 2 * BLOCKS)
        def _():
            load(q + 2).start()

    def swap(b):
        rows = block_rows(b)
        return remote(p_other.at[rows], ex.at[rows], ex_send.at[b], ex_recv.at[b], sibling)

    load(0).start()
    load(1).start()
    g_high[...], g_low[...] = parts_of(g_ref[...])
    multiply(0, p_other)

    if square:
        pl.semaphore_wait(barrier, jnp.where(is_far, 2, 3))
    else:
        pl.semaphore_wait(barrier, jnp.where(is_root, line, 2))

    swap(0).start()
    multiply(1, p_own)

    def rows_of(i):
        return pl.ds(pl.multiple_of(i * chunk, chunk), chunk)

    def own(i):
        return p_own[rows_of(i), :] + ex[rows_of(i), :]

    def up_copy(i):
        return remote(rin.at[rows_of(i)], rin.at[rows_of(i)], z_send.at[i], r_recv.at[i], up)

    def down_copy(i):
        return remote(lin.at[rows_of(i)], lin.at[rows_of(i)], z_send.at[i], l_recv.at[i], down)

    def out_copy(i, sems, target):
        return remote(o_ref.at[rows_of(i)], o_ref.at[rows_of(i)], sems.at[i], o_recv.at[i], target)

    last = jnp.maximum(z, line - 1 - z)

    def within(i):
        return (i >= 0) & (i < CHUNKS)

    def step(t, carry):
        now = t // EACH

        @pl.when((t % EACH == 0) & (now < BLOCKS))
        def _():
            swap(now).wait_recv()

        @pl.when((t % EACH == 0) & (now < BLOCKS - 1))
        def _():
            multiply(2 * now + 2, p_other)
            swap(now + 1).start()

        @pl.when((t % EACH == EACH // 2) & (now < BLOCKS - 1))
        def _():
            multiply(2 * now + 3, p_own)

        i = t - SKEW * z

        @pl.when(within(i) & (z < r))
        def _():
            @pl.when(z == 0)
            def _():
                rin[rows_of(i), :] = own(i)

            @pl.when(z > 0)
            def _():
                up_copy(i).wait_recv()
                rin[rows_of(i), :] = rin[rows_of(i), :] + own(i)

            up_copy(i).start()

        j = t - SKEW * (line - 1 - z)

        @pl.when(within(j) & (z > r))
        def _():
            @pl.when(z == line - 1)
            def _():
                lin[rows_of(j), :] = own(j)

            @pl.when(z < line - 1)
            def _():
                down_copy(j).wait_recv()
                lin[rows_of(j), :] = lin[rows_of(j), :] + own(j)

            down_copy(j).start()

        m = t - SKEW * last

        @pl.when(within(m) & is_root)
        def _():
            o_ref[rows_of(m), :] = own(m)

            @pl.when(z > 0)
            def _():
                up_copy(m).wait_recv()
                o_ref[rows_of(m), :] = o_ref[rows_of(m), :] + rin[rows_of(m), :]

            @pl.when(z < line - 1)
            def _():
                down_copy(m).wait_recv()
                o_ref[rows_of(m), :] = o_ref[rows_of(m), :] + lin[rows_of(m), :]

            if square:
                out_copy(m, a_send, across_x).start()
                out_copy(m, b_send, across_y).start()
            else:
                for n in range(1, line):
                    out_copy(m, more_send[n - 1], {"row": (z + n) % line}).start()

        if square:
            f = m - SKEW

            @pl.when(within(f) & is_x)
            def _():
                out_copy(f, a_send, across_y).wait_recv()

                @pl.when(f % 2 == 0)
                def _():
                    out_copy(f, a_send, across_y).start()

            @pl.when(within(f) & is_y)
            def _():
                out_copy(f, a_send, across_x).wait_recv()

                @pl.when(f % 2 == 1)
                def _():
                    out_copy(f, a_send, across_x).start()

        return carry

    lax.fori_loop(0, CHUNKS + SKEW * line, step, 0)

    for b in range(BLOCKS):
        swap(b).wait_send()

    def finish(i, carry):
        @pl.when(jnp.logical_not(is_root))
        def _():
            up_copy(i).wait_send()

        if square:
            @pl.when(is_root)
            def _():
                out_copy(i, a_send, across_x).wait_send()
                out_copy(i, b_send, across_y).wait_send()

            @pl.when((is_x & (i % 2 == 0)) | (is_y & (i % 2 == 1)))
            def _():
                out_copy(i, a_send, across_y).wait_send()

            @pl.when(is_far)
            def _():
                out_copy(i, a_send, across_y).wait_recv()
        else:
            @pl.when(is_root)
            def _():
                for n in range(1, line):
                    out_copy(i, more_send[n - 1], {"row": (z + n) % line}).wait_send()

            @pl.when(jnp.logical_not(is_root))
            def _():
                out_copy(i, more_send[0], {"row": z}).wait_recv()

        return carry

    lax.fori_loop(0, CHUNKS, finish, 0)


def collect(gram, matrix, line):
    depth, cols = gram.shape
    half = matrix.shape[0] // 2
    chunk = half // CHUNKS
    buffer = pltpu.VMEM((half, cols), jnp.float32)
    extra = 0 if line == 4 else line - 1
    return pl.pallas_call(
        functools.partial(collect_kernel, line, chunk),
        out_shape=jax.ShapeDtypeStruct((half, cols), jnp.float32),
        in_specs=[pl.BlockSpec(memory_space=pltpu.VMEM), pl.BlockSpec(memory_space=pl.ANY)],
        out_specs=pl.BlockSpec(memory_space=pltpu.VMEM),
        scratch_shapes=[
            pltpu.VMEM((2, EACH * chunk, depth), jnp.float32),
            pltpu.SemaphoreType.DMA((2,)),
        ]
        + [pltpu.VMEM((depth, cols), jnp.bfloat16)] * 2
        + [buffer] * 5
        + [pltpu.SemaphoreType.DMA((BLOCKS,))] * 2
        + [pltpu.SemaphoreType.DMA((CHUNKS,))] * (6 + extra),
        compiler_params=pltpu.CompilerParams(
            collective_id=2, has_side_effects=True, vmem_limit_bytes=VMEM_LIMIT
        ),
        cost_estimate=pl.CostEstimate(
            flops=12 * half * cols * depth, bytes_accessed=220 * 1000000, transcendentals=0
        ),
        name="collect_product",
    )(gram, matrix)


def product(a, b, dims):
    return lax.dot_general(
        a, b, (dims, ((), ())), precision=lax.Precision.HIGH, preferred_element_type=jnp.float32
    )


def identity_rows(first, count, start, width):
    rows_global = first + jnp.arange(count, dtype=jnp.int32)
    return (rows_global[:, None] == start + jnp.arange(width, dtype=jnp.int32)[None, :]).astype(
        jnp.float32
    )


def per_device(matrix, factor_inverse, panel, split_index):
    cols_loc = matrix.shape[1]
    width = factor_inverse.shape[0]
    ncol = lax.axis_size("col")
    line = lax.axis_size("row")
    assert ncol == 2 * line
    order = cols_loc * ncol
    col_idx = lax.axis_index("col")
    start = panel[0] * width
    owner = start // cols_loc
    offset = start - owner * cols_loc
    group = width // GROUPS

    partials, grams, collected = [], [], []
    for g in range(GROUPS):
        piece = lax.dynamic_slice_in_dim(matrix, offset + g * group, group, 1)
        piece = jnp.where(owner == col_idx, piece, jnp.float32(0.0))
        if partials:
            piece, partials[-1] = lax.optimization_barrier((piece, partials[-1]))
        partials.append(spread(piece, matrix, line))
    for g in range(GROUPS):
        if grams:
            partials[g], grams[-1] = lax.optimization_barrier((partials[g], grams[-1]))
        grams.append(
            lax.psum(partials[g], "row").T / order
            + identity_rows(col_idx * cols_loc, cols_loc, start + g * group, group)
        )
    for g in range(GROUPS):
        collected.append(collect(grams[g], matrix, line))
    total = product(jnp.concatenate(collected, axis=1), factor_inverse, ((1,), (1,)))
    col_rows = order // ncol
    projector = 0.5 * (identity_rows(col_idx * col_rows, col_rows, start, width) + total)
    rows_global = col_idx * col_rows + jnp.arange(col_rows, dtype=jnp.int32)
    keep = (rows_global < order // 2) == (rows_global < split_index[0])
    return jnp.where(keep[:, None], projector, jnp.float32(0.0))


def solution(mesh):
    placed = (P("row", "col"), P(), P(), P())
    return jax.shard_map(
        per_device, mesh=mesh, in_specs=placed, out_specs=P("col", None), check_vma=False
    )
```

```python
import functools

import jax
import jax.numpy as jnp
from jax import lax
from jax.experimental import pallas as pl
from jax.experimental.pallas import tpu as pltpu
from jax.sharding import PartitionSpec as P

GROUPS = 2
CHUNKS = 32
SKEW = 2
BLOCKS = 8
EACH = CHUNKS // BLOCKS
VMEM_LIMIT = 40 * 1024 * 1024


def remote(src, dst, send, recv, target):
    return pltpu.make_async_remote_copy(
        src_ref=src,
        dst_ref=dst,
        send_sem=send,
        recv_sem=recv,
        device_id=target,
        device_id_type=pl.DeviceIdType.MESH,
    )


def signal(barrier, target):
    pl.semaphore_signal(barrier, inc=1, device_id=target, device_id_type=pl.DeviceIdType.MESH)


def parts_of(x):
    high = x.astype(jnp.bfloat16)
    return high, (x - high.astype(jnp.float32)).astype(jnp.bfloat16)


def split_dot(a, b):
    total = jnp.dot(a[1], b[0], preferred_element_type=jnp.float32)
    total = total + jnp.dot(a[0], b[1], preferred_element_type=jnp.float32)
    return total + jnp.dot(a[0], b[0], preferred_element_type=jnp.float32)


def spread_kernel(
    line, chunk, x_ref, a_ref, g_ref, o_ref, a_buf, a_sem, ex, rin, lin,
    ex_send, ex_recv, r_send, r_recv, l_send, l_recv, s_send, s_recv,
):
    c = lax.axis_index("col")
    z = c // 2
    k = c % 2
    half = CHUNKS * chunk
    base = pl.multiple_of(k * half, half)
    other = pl.multiple_of((1 - k) * half, half)
    sibling, up, down = {"col": c + 1 - 2 * k}, {"col": c + 2}, {"col": c - 2}
    has_down, has_up = z > 0, z < line - 1

    barrier = pltpu.get_barrier_semaphore()
    signal(barrier, sibling)

    @pl.when(has_down)
    def _():
        signal(barrier, down)

    @pl.when(has_up)
    def _():
        signal(barrier, up)

    block = EACH * chunk

    def block_rows(q):
        half_no = (k + q) % 2
        return pl.ds(pl.multiple_of(half_no * half + (q // 2) * block, block), block)

    def load(q):
        slot = q % 2
        return pltpu.make_async_copy(a_ref.at[block_rows(q)], a_buf.at[slot], a_sem.at[slot])

    load(0).start()
    load(1).start()
    g_ref[...] = jnp.zeros_like(g_ref)

    pl.semaphore_wait(barrier, 1 + has_down.astype(jnp.int32) + has_up.astype(jnp.int32))

    def accumulate(q):
        load(q).wait()
        panel = parts_of(jnp.transpose(o_ref[block_rows(q), :]))
        g_ref[...] += split_dot(panel, parts_of(a_buf[q % 2]))

        @pl.when(q + 2 < 2 * BLOCKS)
        def _():
            load(q + 2).start()

    def swap(b):
        rows = pl.ds(pl.multiple_of(b * block, block), block)
        source = pl.ds(pl.multiple_of(other + b * block, block), block)
        return remote(x_ref.at[source], ex.at[rows], ex_send.at[b], ex_recv.at[b], sibling)

    for b in range(BLOCKS):
        swap(b).start()

    def rows_of(i):
        return pl.ds(pl.multiple_of(i * chunk, chunk), chunk)

    def whole_rows(i):
        return pl.ds(pl.multiple_of(base + i * chunk, chunk), chunk)

    def up_copy(i):
        return remote(rin.at[rows_of(i)], rin.at[rows_of(i)], r_send.at[i], r_recv.at[i], up)

    def down_copy(i):
        return remote(lin.at[rows_of(i)], lin.at[rows_of(i)], l_send.at[i], l_recv.at[i], down)

    def side_copy(i):
        return remote(
            o_ref.at[whole_rows(i)], o_ref.at[whole_rows(i)], s_send.at[i], s_recv.at[i], sibling
        )

    def side_wait(i):
        rows = pl.ds(pl.multiple_of(other + i * chunk, chunk), chunk)
        remote(o_ref.at[rows], o_ref.at[rows], s_send.at[i], s_recv.at[i], sibling).wait_recv()

    def accumulate_side(b):
        def wait_one(n, carry):
            side_wait(b * EACH + n)
            return carry

        lax.fori_loop(0, EACH, wait_one, 0)
        accumulate(2 * b + 1)

    def own(i):
        return x_ref[whole_rows(i), :] + ex[rows_of(i), :]

    last = jnp.maximum(z, line - 1 - z)

    def step(t, carry):
        @pl.when((t % EACH == 0) & (t < CHUNKS))
        def _():
            swap(t // EACH).wait_recv()

        i = t - SKEW * z

        @pl.when((i >= 0) & (i < CHUNKS))
        def _():
            @pl.when(z == 0)
            def _():
                rin[rows_of(i), :] = own(i)

            @pl.when(has_down)
            def _():
                up_copy(i).wait_recv()
                rin[rows_of(i), :] = rin[rows_of(i), :] + own(i)

            @pl.when(has_up)
            def _():
                up_copy(i).start()

        j = t - SKEW * (line - 1 - z)

        @pl.when((j >= 0) & (j < CHUNKS))
        def _():
            @pl.when(z == line - 1)
            def _():
                lin[rows_of(j), :] = own(j)

            @pl.when(has_up)
            def _():
                down_copy(j).wait_recv()
                lin[rows_of(j), :] = lin[rows_of(j), :] + own(j)

            @pl.when(has_down)
            def _():
                down_copy(j).start()

        m = t - SKEW * last

        @pl.when((m >= 0) & (m < CHUNKS))
        def _():
            o_ref[whole_rows(m), :] = (rin[rows_of(m), :] + lin[rows_of(m), :]) - own(m)
            side_copy(m).start()

            @pl.when(m % EACH == EACH - 1)
            def _():
                accumulate(2 * (m // EACH))

            @pl.when((m % EACH == EACH // 2 - 1) & (m >= EACH))
            def _():
                accumulate_side(m // EACH - 1)

        return carry

    lax.fori_loop(0, CHUNKS + SKEW * (line - 1), step, 0)

    accumulate_side(BLOCKS - 1)
    for b in range(BLOCKS):
        swap(b).wait_send()

    def finish(i, carry):
        @pl.when(has_up)
        def _():
            up_copy(i).wait_send()

        @pl.when(has_down)
        def _():
            down_copy(i).wait_send()

        side_copy(i).wait_send()
        return carry

    lax.fori_loop(0, CHUNKS, finish, 0)


def spread(x, matrix, line):
    rows, cols = x.shape
    depth = matrix.shape[1]
    half = rows // 2
    chunk = half // CHUNKS
    buffer = pltpu.VMEM((half, cols), jnp.float32)
    return pl.pallas_call(
        functools.partial(spread_kernel, line, chunk),
        out_shape=jax.ShapeDtypeStruct((cols, depth), jnp.float32),
        in_specs=[pl.BlockSpec(memory_space=pltpu.VMEM), pl.BlockSpec(memory_space=pl.ANY)],
        out_specs=pl.BlockSpec(memory_space=pltpu.VMEM),
        scratch_shapes=[
            pltpu.VMEM((rows, cols), jnp.float32),
            pltpu.VMEM((2, EACH * chunk, depth), jnp.float32),
            pltpu.SemaphoreType.DMA((2,)),
        ]
        + [buffer] * 3
        + [pltpu.SemaphoreType.DMA((BLOCKS,))] * 2
        + [pltpu.SemaphoreType.DMA((CHUNKS,))] * 6,
        compiler_params=pltpu.CompilerParams(
            collective_id=1, has_side_effects=True, vmem_limit_bytes=VMEM_LIMIT
        ),
        cost_estimate=pl.CostEstimate(
            flops=6 * rows * cols * depth, bytes_accessed=220 * 1000000, transcendentals=0
        ),
        name="spread_panel",
    )(x, matrix)


def collect_kernel(
    line, chunk, g_ref, a_ref, o_ref, a_buf, a_sem, g_high, g_low, p_own, p_other, ex, rin, lin,
    ex_send, ex_recv, z_send, r_recv, l_recv, a_send, b_send, o_recv, *more_send,
):
    r = lax.axis_index("row")
    c = lax.axis_index("col")
    z = c // 2
    k = c % 2
    half = CHUNKS * chunk
    base = pl.multiple_of(k * half, half)
    other = pl.multiple_of((1 - k) * half, half)
    sibling, up, down = {"col": c + 1 - 2 * k}, {"col": c + 2}, {"col": c - 2}
    square = line == 4
    is_root = r == z
    if square:
        across_x, across_y = {"row": r + 1 - 2 * (r % 2)}, {"row": r + 2 - 4 * (r // 2)}
        same_x, same_y = (r % 2) == (z % 2), (r // 2) == (z // 2)
        is_x = jnp.logical_not(same_x) & same_y
        is_y = same_x & jnp.logical_not(same_y)
        is_far = jnp.logical_not(same_x) & jnp.logical_not(same_y)

    barrier = pltpu.get_barrier_semaphore()
    signal(barrier, sibling)

    @pl.when((z > 0) & (z <= r))
    def _():
        signal(barrier, down)

    @pl.when((z < line - 1) & (z >= r))
    def _():
        signal(barrier, up)

    if square:
        @pl.when(is_x | is_far)
        def _():
            signal(barrier, across_x)

        @pl.when(is_y | is_far)
        def _():
            signal(barrier, across_y)
    else:
        @pl.when(jnp.logical_not(is_root))
        def _():
            signal(barrier, {"row": z})

    block = EACH * chunk

    def load(q):
        slot = q % 2
        first = ((1 - k + q) % 2) * half + (q // 2) * block
        rows = pl.ds(pl.multiple_of(first, block), block)
        return pltpu.make_async_copy(a_ref.at[rows], a_buf.at[slot], a_sem.at[slot])

    def block_rows(b):
        return pl.ds(pl.multiple_of(b * block, block), block)

    def multiply(q, target):
        load(q).wait()
        target[block_rows(q // 2), :] = split_dot(
            parts_of(a_buf[q % 2]), (g_high[...], g_low[...])
        )

        @pl.when(q + 2 < 2 * BLOCKS)
        def _():
            load(q + 2).start()

    def swap(b):
        rows = block_rows(b)
        return remote(p_other.at[rows], ex.at[rows], ex_send.at[b], ex_recv.at[b], sibling)

    load(0).start()
    load(1).start()
    g_high[...], g_low[...] = parts_of(g_ref[...])
    multiply(0, p_other)

    if square:
        pl.semaphore_wait(barrier, jnp.where(is_far, 2, 3))
    else:
        pl.semaphore_wait(barrier, jnp.where(is_root, line, 2))

    swap(0).start()
    multiply(1, p_own)

    def rows_of(i):
        return pl.ds(pl.multiple_of(i * chunk, chunk), chunk)

    def own(i):
        return p_own[rows_of(i), :] + ex[rows_of(i), :]

    def up_copy(i):
        return remote(rin.at[rows_of(i)], rin.at[rows_of(i)], z_send.at[i], r_recv.at[i], up)

    def down_copy(i):
        return remote(lin.at[rows_of(i)], lin.at[rows_of(i)], z_send.at[i], l_recv.at[i], down)

    def out_copy(i, sems, target):
        return remote(o_ref.at[rows_of(i)], o_ref.at[rows_of(i)], sems.at[i], o_recv.at[i], target)

    last = jnp.maximum(z, line - 1 - z)

    def within(i):
        return (i >= 0) & (i < CHUNKS)

    def step(t, carry):
        now = t // EACH

        @pl.when((t % EACH == 0) & (now < BLOCKS))
        def _():
            swap(now).wait_recv()

        @pl.when((t % EACH == 0) & (now < BLOCKS - 1))
        def _():
            multiply(2 * now + 2, p_other)
            swap(now + 1).start()

        @pl.when((t % EACH == EACH // 2) & (now < BLOCKS - 1))
        def _():
            multiply(2 * now + 3, p_own)

        i = t - SKEW * z

        @pl.when(within(i) & (z < r))
        def _():
            @pl.when(z == 0)
            def _():
                rin[rows_of(i), :] = own(i)

            @pl.when(z > 0)
            def _():
                up_copy(i).wait_recv()
                rin[rows_of(i), :] = rin[rows_of(i), :] + own(i)

            up_copy(i).start()

        j = t - SKEW * (line - 1 - z)

        @pl.when(within(j) & (z > r))
        def _():
            @pl.when(z == line - 1)
            def _():
                lin[rows_of(j), :] = own(j)

            @pl.when(z < line - 1)
            def _():
                down_copy(j).wait_recv()
                lin[rows_of(j), :] = lin[rows_of(j), :] + own(j)

            down_copy(j).start()

        m = t - SKEW * last

        @pl.when(within(m) & is_root)
        def _():
            o_ref[rows_of(m), :] = own(m)

            @pl.when(z > 0)
            def _():
                up_copy(m).wait_recv()
                o_ref[rows_of(m), :] = o_ref[rows_of(m), :] + rin[rows_of(m), :]

            @pl.when(z < line - 1)
            def _():
                down_copy(m).wait_recv()
                o_ref[rows_of(m), :] = o_ref[rows_of(m), :] + lin[rows_of(m), :]

            if square:
                out_copy(m, a_send, across_x).start()
                out_copy(m, b_send, across_y).start()
            else:
                for n in range(1, line):
                    out_copy(m, more_send[n - 1], {"row": (z + n) % line}).start()

        if square:
            f = m - SKEW

            @pl.when(within(f) & is_x)
            def _():
                out_copy(f, a_send, across_y).wait_recv()

                @pl.when(f % 2 == 0)
                def _():
                    out_copy(f, a_send, across_y).start()

            @pl.when(within(f) & is_y)
            def _():
                out_copy(f, a_send, across_x).wait_recv()

                @pl.when(f % 2 == 1)
                def _():
                    out_copy(f, a_send, across_x).start()

        return carry

    lax.fori_loop(0, CHUNKS + SKEW * line, step, 0)

    for b in range(BLOCKS):
        swap(b).wait_send()

    def finish(i, carry):
        @pl.when(jnp.logical_not(is_root))
        def _():
            up_copy(i).wait_send()

        if square:
            @pl.when(is_root)
            def _():
                out_copy(i, a_send, across_x).wait_send()
                out_copy(i, b_send, across_y).wait_send()

            @pl.when((is_x & (i % 2 == 0)) | (is_y & (i % 2 == 1)))
            def _():
                out_copy(i, a_send, across_y).wait_send()

            @pl.when(is_far)
            def _():
                out_copy(i, a_send, across_y).wait_recv()
        else:
            @pl.when(is_root)
            def _():
                for n in range(1, line):
                    out_copy(i, more_send[n - 1], {"row": (z + n) % line}).wait_send()

            @pl.when(jnp.logical_not(is_root))
            def _():
                out_copy(i, more_send[0], {"row": z}).wait_recv()

        return carry

    lax.fori_loop(0, CHUNKS, finish, 0)


def collect(gram, matrix, line):
    depth, cols = gram.shape
    half = matrix.shape[0] // 2
    chunk = half // CHUNKS
    buffer = pltpu.VMEM((half, cols), jnp.float32)
    extra = 0 if line == 4 else line - 1
    return pl.pallas_call(
        functools.partial(collect_kernel, line, chunk),
        out_shape=jax.ShapeDtypeStruct((half, cols), jnp.float32),
        in_specs=[pl.BlockSpec(memory_space=pltpu.VMEM), pl.BlockSpec(memory_space=pl.ANY)],
        out_specs=pl.BlockSpec(memory_space=pltpu.VMEM),
        scratch_shapes=[
            pltpu.VMEM((2, EACH * chunk, depth), jnp.float32),
            pltpu.SemaphoreType.DMA((2,)),
        ]
        + [pltpu.VMEM((depth, cols), jnp.bfloat16)] * 2
        + [buffer] * 5
        + [pltpu.SemaphoreType.DMA((BLOCKS,))] * 2
        + [pltpu.SemaphoreType.DMA((CHUNKS,))] * (6 + extra),
        compiler_params=pltpu.CompilerParams(
            collective_id=2, has_side_effects=True, vmem_limit_bytes=VMEM_LIMIT
        ),
        cost_estimate=pl.CostEstimate(
            flops=12 * half * cols * depth, bytes_accessed=220 * 1000000, transcendentals=0
        ),
        name="collect_product",
    )(gram, matrix)


def product(a, b, dims):
    return lax.dot_general(
        a, b, (dims, ((), ())), precision=lax.Precision.HIGH, preferred_element_type=jnp.float32
    )


def identity_rows(first, count, start, width):
    rows_global = first + jnp.arange(count, dtype=jnp.int32)
    return (rows_global[:, None] == start + jnp.arange(width, dtype=jnp.int32)[None, :]).astype(
        jnp.float32
    )


def per_device(matrix, factor_inverse, panel, split_index):
    cols_loc = matrix.shape[1]
    width = factor_inverse.shape[0]
    ncol = lax.axis_size("col")
    line = lax.axis_size("row")
    assert ncol == 2 * line
    order = cols_loc * ncol
    col_idx = lax.axis_index("col")
    start = panel[0] * width
    owner = start // cols_loc
    offset = start - owner * cols_loc
    group = width // GROUPS

    partials, grams, collected = [], [], []
    for g in range(GROUPS):
        piece = lax.dynamic_slice_in_dim(matrix, offset + g * group, group, 1)
        piece = jnp.where(owner == col_idx, piece, jnp.float32(0.0))
        if partials:
            piece, partials[-1] = lax.optimization_barrier((piece, partials[-1]))
        partials.append(spread(piece, matrix, line))
    for g in range(GROUPS):
        if grams:
            partials[g], grams[-1] = lax.optimization_barrier((partials[g], grams[-1]))
        grams.append(
            lax.psum(partials[g], "row").T / order
            + identity_rows(col_idx * cols_loc, cols_loc, start + g * group, group)
        )
    for g in range(GROUPS):
        collected.append(collect(grams[g], matrix, line))
    total = product(jnp.concatenate(collected, axis=1), factor_inverse, ((1,), (1,)))
    col_rows = order // ncol
    projector = 0.5 * (identity_rows(col_idx * col_rows, col_rows, start, width) + total)
    rows_global = col_idx * col_rows + jnp.arange(col_rows, dtype=jnp.int32)
    keep = (rows_global < order // 2) == (rows_global < split_index[0])
    return jnp.where(keep[:, None], projector, jnp.float32(0.0))


def solution(mesh):
    placed = (P("row", "col"), P(), P(), P())
    return jax.shard_map(
        per_device, mesh=mesh, in_specs=placed, out_specs=P("col", None), check_vma=False
    )
```
